256 devices in a mesh: gx: 32 (over z, y_hi, core), gy: 8 (over x, y_lo).
Axes of the slice: x: 4, y: 4 (y_hi: 2, y_lo: 2; y = y_hi * 2 + y_lo), z: 8, core: 2. Of those that a mesh axis runs over, the one named last changes fastest.
Arguments:
- courant: float32 [512, 128, 256], P('gx', 'gy'), may hold values from 0.05 to 0.18
- vel_entering: float32 [16, 128, 256], P(None, 'gy'), may hold values from 0.05 to 0.18
- image: float32 [512, 128, 256], P('gx', 'gy'), may hold values from -6 to 6
- src_prev: float32 [512, 128, 256], P('gx', 'gy'), may hold values from -6 to 6
- src_cur: float32 [512, 128, 256], P('gx', 'gy'), may hold values from -6 to 6
- rcv_prev: float32 [512, 128, 256], P('gx', 'gy'), may hold values from -6 to 6
- rcv_cur: float32 [512, 128, 256], P('gx', 'gy'), may hold values from -6 to 6
- global_image: float32 [512, 128, 256], P('gx', 'gy'), may hold values from -6 to 6
- shift_map: int32 [128], P('gy'), may hold values from 0 to 1, as said below
- image_owner: int32 [8, 32], P('gy'), may hold values from 0 to 31, each once within a row
Outputs:
- global_out: float32 [512, 128, 256], P('gx', 'gy')
- image_out: float32 [512, 128, 256], P('gx', 'gy')
- src_prev_out: float32 [512, 128, 256], P('gx', 'gy')
- src_cur_out: float32 [512, 128, 256], P('gx', 'gy')
- rcv_prev_out: float32 [512, 128, 256], P('gx', 'gy')
- rcv_cur_out: float32 [512, 128, 256], P('gx', 'gy')
The draws below stay inside these ranges and needn't reach their ends.
Inputs may be any that keep to these rules, and one draw needn't show every extreme that they name: `shift_map`: exactly 64 crosslines move, which ones varies. Each row of image_owner names every index along gx once.
All inputs are finite; a program needn't handle non-finite values.
Results may differ from the reference program's by a relative error of at most 0.00002.
Values sent between devices are 32-bit elements; how exact they have to be, the bound alone decides.
No kernel may reach another device: no remote copies, remote signals or barrier semaphores. Data moves between devices by JAX's collectives and lax.ppermute only.
A program may use at most 64 MiB of HBM per device.

```python
import math
import jax
import jax.numpy as jnp

CX = 16
CY = 16
STEPS = 4
NX = 512
NY = 128
NZ = 256
ROWS = 8
N_GX = 32


def draw_shift_map(key, part):
    key = jax.random.fold_in(key, 11)
    ordering = jax.random.permutation(key, NY)
    return (ordering < NY // 2).astype(jnp.int32)


def level_of(stream_key, dims, shards, low, largest):
    loudness, own = 1.0, jax.random.fold_in(stream_key, 6)
    for axis_at, shards_of in shards:
        draws = jnp.exp(jax.random.uniform(jax.random.fold_in(own, axis_at), (shards_of,), jnp.float32, low / len(shards), largest / len(shards)))
        loudness = loudness * jnp.repeat(draws, dims[axis_at] // shards_of).reshape([-1 if axis == axis_at else 1 for axis in range(len(dims))])
    return loudness


def noise(own_key, shape, deviation, most, pieces=(), held_as=jnp.bfloat16):
    array = jax.random.normal(own_key, shape, jnp.float32) * deviation
    if len(pieces) > 0:
        array = level_of(own_key, shape, pieces, -0.22, 0.18) * array
    return jnp.clip(array, min=-most, max=most).astype(held_as)


def setup_inputs(seed: int = 0) -> dict:
    key_of = jax.random.split(jax.random.key(seed), 11)
    courant = jnp.clip(jnp.exp(math.log(0.18) - 1.2809339 * jax.random.uniform(key_of[0], (NX, NY, NZ), jnp.float32) ** level_of(key_of[0], (NX, NY, NZ), ((0, 32), (1, 8)), -0.2, 0.2)), 0.05, 0.18)
    vel_entering = jnp.clip(jnp.exp(math.log(0.18) - 1.2809339 * jax.random.uniform(key_of[1], (CX, NY, NZ), jnp.float32) ** level_of(key_of[1], (CX, NY, NZ), ((1, 8),), -0.2, 0.2)), 0.05, 0.18)
    image = noise(key_of[2], (NX, NY, NZ), 1.0, 6.0, ((0, 32), (1, 8)), jnp.float32)
    src_prev = noise(key_of[3], (NX, NY, NZ), 1.0, 6.0, ((0, 32), (1, 8)), jnp.float32)
    src_cur = noise(key_of[4], (NX, NY, NZ), 1.0, 6.0, ((0, 32), (1, 8)), jnp.float32)
    rcv_prev = noise(key_of[5], (NX, NY, NZ), 1.0, 6.0, ((0, 32), (1, 8)), jnp.float32)
    rcv_cur = noise(key_of[6], (NX, NY, NZ), 1.0, 6.0, ((0, 32), (1, 8)), jnp.float32)
    global_image = noise(key_of[7], (NX, NY, NZ), 1.0, 6.0, ((0, 32), (1, 8)), jnp.float32)
    shift_map = draw_shift_map(jax.random.fold_in(key_of[10], 71), 0)
    image_owner = jax.vmap(lambda own: jax.random.permutation(own, N_GX))(jax.random.split(key_of[9], ROWS)).reshape((ROWS, N_GX)).astype(jnp.int32)
    return {"courant": courant, "vel_entering": vel_entering, "image": image, "src_prev": src_prev, "src_cur": src_cur, "rcv_prev": rcv_prev, "rcv_cur": rcv_cur, "global_image": global_image, "shift_map": shift_map, "image_owner": image_owner}


STENCIL = (-205.0 / 72.0, 8.0 / 5.0, -1.0 / 5.0, 8.0 / 315.0, -1.0 / 560.0)


def shifted_view(padded, which_axis, reach):
    leading = padded.ndim - 3
    selector = [slice(None)] * padded.ndim
    for each_axis in range(3):
        extent = padded.shape[leading + each_axis]
        displacement = reach if each_axis == which_axis else 0
        selector[leading + each_axis] = slice(4 + displacement, extent - 4 + displacement)
    return padded[tuple(selector)]


def laplace(padded):
    accumulated = (3.0 * STENCIL[0]) * shifted_view(padded, 0, 0)
    for reach in range(1, 5):
        for which_axis in range(3):
            accumulated = accumulated + STENCIL[reach] * (shifted_view(padded, which_axis, reach) + shifted_view(padded, which_axis, -reach))
    return accumulated


def reference(courant, vel_entering, image, src_prev, src_cur, rcv_prev, rcv_cur, global_image, shift_map, image_owner):
    row_moved = (shift_map == 1)[None, :, None]
    zeros_tile = jnp.zeros((CX, NY, NZ), jnp.float32)

    def advance(field, entering):
        return jnp.where(row_moved, jnp.concatenate([field[CX:], entering], axis=0), field)

    departing = jnp.where(row_moved, image[:CX], jnp.float32(0.0))
    owner_grid = jnp.repeat(jnp.repeat(image_owner, CY, axis=0), NZ // N_GX, axis=1)
    owner_cells = (jnp.arange(N_GX, dtype=jnp.int32)[:, None, None] == owner_grid[None])[:, None]
    blocks = global_image.reshape(N_GX, CX, NY, NZ)
    global_out = jnp.where(owner_cells, blocks + departing[None], blocks).reshape(NX, NY, NZ)

    velocity = advance(courant, vel_entering)
    picture = advance(image, zeros_tile)
    source_prev = advance(src_prev, zeros_tile)
    source_cur = advance(src_cur, zeros_tile)
    receiver_prev = advance(rcv_prev, zeros_tile)
    receiver_cur = advance(rcv_cur, zeros_tile)
    for step_index in range(STEPS):
        source_next = 2.0 * source_cur - source_prev + velocity * laplace(jnp.pad(source_cur, 4))
        receiver_next = 2.0 * receiver_cur - receiver_prev + velocity * laplace(jnp.pad(receiver_cur, 4))
        source_prev, source_cur = source_cur, source_next
        receiver_prev, receiver_cur = receiver_cur, receiver_next
        picture = picture + source_cur * receiver_cur
    return global_out, picture, source_prev, source_cur, receiver_prev, receiver_cur
```

```python
import functools

import jax
import jax.numpy as jnp
from jax import lax
from jax.experimental import pallas as pl
from jax.experimental.pallas import tpu as pltpu
from jax.sharding import PartitionSpec as P

STEPS = 4
STENCIL = (-205.0 / 72.0, 8.0 / 5.0, -1.0 / 5.0, 8.0 / 315.0, -1.0 / 560.0)
F32 = jnp.float32
HIGHEST = lax.Precision.HIGHEST


def sds(*shape):
    return jax.ShapeDtypeStruct(shape, F32)


def call(kernel, outs, scratch, flops, *args):
    specs = [
        pl.BlockSpec(memory_space=pltpu.SMEM if a.ndim == 1 else pltpu.VMEM) for a in args
    ]
    return pl.pallas_call(
        kernel,
        out_shape=outs,
        in_specs=specs,
        out_specs=[pl.BlockSpec(memory_space=pltpu.VMEM)] * len(outs),
        scratch_shapes=scratch,
        compiler_params=pltpu.CompilerParams(vmem_limit_bytes=24 * 1024 * 1024),
        cost_estimate=pl.CostEstimate(flops=flops, bytes_accessed=1 << 20, transcendentals=0),
    )(*args)


def send_faces(here, fields, sends):
    x1, od, y1, yo = sends
    even_x, even_y = lax.rem(here[0], 2) == 0, lax.rem(here[1], 2) == 0
    toward = jnp.where(even_x, 12, 0)
    for f, field in enumerate(fields):
        x1[f] = field[pl.ds(toward, 4)]
        od[f] = field[pl.ds(12 - toward, 4)]
        for half in range(2):
            block = field[8 * half : 8 * half + 8]
            low, high = block[:, 0:4, :], block[:, 12:16, :]
            rows = slice(4 * half, 4 * half + 4)
            y1[f, :, rows, :] = jnp.where(even_y, high, low)
            yo[f, :, rows, :] = jnp.where(even_y, low, high)


def extend(here, field, halos, f, ext):
    x1, od, y1, yo = halos
    gx, gy = here[0], here[1]
    even_x, even_y = lax.rem(gx, 2) == 0, lax.rem(gy, 2) == 0
    zero = F32(0.0)
    ext[4:20, 8:24, :] = field[...]
    a, b = x1[f], od[f]
    ext[0:4, 8:24, :] = jnp.where(gx > 0, jnp.where(even_x, b, a), zero)
    ext[20:24, 8:24, :] = jnp.where(gx < 31, jnp.where(even_x, a, b), zero)
    a, b = y1[f], yo[f]
    low = jnp.where(gy > 0, jnp.where(even_y, b, a), zero)
    high = jnp.where(gy < 7, jnp.where(even_y, a, b), zero)
    for half in range(2):
        rows = slice(4 * half, 4 * half + 4)
        xs = slice(4 + 8 * half, 12 + 8 * half)
        ext[xs, 4:8, :] = low[:, rows, :]
        ext[xs, 24:28, :] = high[:, rows, :]


def depth_matrix():
    i = lax.broadcasted_iota(jnp.int32, (256, 256), 0)
    j = lax.broadcasted_iota(jnp.int32, (256, 256), 1)
    apart = jnp.abs(i - j)
    m = jnp.where(apart == 0, F32(3.0 * STENCIL[0]), F32(0.0))
    for k in range(1, 5):
        m = jnp.where(apart == k, F32(STENCIL[k]), m)
    return m


def advance(field, prev_of, vel, ext, depth, out):
    for x in range(0, 16, 2):
        lap = depth[x : x + 2]
        for k in range(1, 5):
            pair = ext[4 + x + k : 6 + x + k, 8:24, :] + ext[4 + x - k : 6 + x - k, 8:24, :]
            pair = pair + (ext[4 + x : 6 + x, 8 + k : 24 + k, :] + ext[4 + x : 6 + x, 8 - k : 24 - k, :])
            lap = lap + F32(STENCIL[k]) * pair
        out[x : x + 2] = 2.0 * field[x : x + 2] - prev_of(x) + vel[x : x + 2] * lap


def move_kernel(here, moves, s, r, s_in, r_in, s_out, r_out, *sends):
    arrives = here[0] < 31
    moved = moves[...] == 1
    for own, come, out in ((s, s_in, s_out), (r, r_in, r_out)):
        for x in range(0, 16, 2):
            out[x : x + 2] = jnp.where(
                moved[None], jnp.where(arrives, come[x : x + 2], F32(0.0)), own[x : x + 2]
            )
    send_faces(here, (s_out, r_out), sends)


def step_kernel(step, *refs):
    refs = list(refs)
    take = lambda n: [refs.pop(0) for _ in range(n)]
    (here,) = take(1)
    s, r = take(2)
    halos = take(4)
    if step == 0:
        moves, s_prev, r_prev, vel_own, vel_end, come = take(6)
    else:
        s_prev, r_prev, vel, picture = take(4)
    if step == STEPS - 1:
        moves, image, image_come = take(3)
    s_out, r_out, picture_out = take(3)
    if step < STEPS - 1:
        sends = take(4)
    if step == 0:
        (vel,) = take(1)
    ext_s, ext_r, depth_s, depth_r = take(4)

    if step in (0, STEPS - 1):
        moved = (moves[...] == 1)[None]
        arrives = here[0] < 31
    if step == 0:
        for x in range(0, 16, 2):
            new = jnp.where(arrives, come[2, x : x + 2], vel_end[x : x + 2])
            vel[x : x + 2] = jnp.where(moved, new, vel_own[x : x + 2])
    matrix = depth_matrix()
    for f, (field, prev, ext, depth, out) in enumerate(
        ((s, s_prev, ext_s, depth_s, s_out), (r, r_prev, ext_r, depth_r, r_out))
    ):
        extend(here, field, halos, f, ext)
        flat = field[...].reshape(256, 256)
        depth[...] = jnp.dot(
            flat, matrix, precision=HIGHEST, preferred_element_type=F32
        ).reshape(16, 16, 256)
        if step == 0:
            prev_of = lambda x, f=f, prev=prev: jnp.where(
                moved, jnp.where(arrives, come[f, x : x + 2], F32(0.0)), prev[x : x + 2]
            )
        else:
            prev_of = lambda x, prev=prev: prev[x : x + 2]
        advance(field, prev_of, vel, ext, depth, out)
    for x in range(0, 16, 2):
        product = s_out[x : x + 2] * r_out[x : x + 2]
        if step > 0:
            product = picture[x : x + 2] + product
        if step == STEPS - 1:
            product = product + jnp.where(
                moved, jnp.where(arrives, image_come[x : x + 2], F32(0.0)), image[x : x + 2]
            )
        picture_out[x : x + 2] = product
    if step < STEPS - 1:
        send_faces(here, (s_out, r_out), sends)


def scatter_kernel(moves, target, image, out):
    rows = lax.broadcasted_iota(jnp.int32, (256, 256), 0)
    pick = jnp.where(rows == target[0:1, :], F32(1.0), F32(0.0))
    leaving = jnp.where((moves[...] == 1)[None], image[...], F32(0.0)).reshape(256, 256)
    out[...] = lax.dot_general(
        pick, leaving, (((1,), (1,)), ((), ())), precision=HIGHEST, preferred_element_type=F32
    )


def gather_kernel(slab, source, base, out):
    rows = lax.broadcasted_iota(jnp.int32, (8, 256), 0)
    place = jnp.where(rows == source[...], F32(1.0), F32(0.0))
    out[...] = base[...] + lax.dot_general(
        slab[...], place, (((0,), (0,)), ((), ())), precision=HIGHEST, preferred_element_type=F32
    ).reshape(16, 16, 256)


def body(
    courant,
    vel_entering,
    image,
    src_prev,
    src_cur,
    rcv_prev,
    rcv_cur,
    global_image,
    shift_map,
    image_owner,
):
    gx, gy = lax.axis_index("gx"), lax.axis_index("gy")
    here = jnp.stack([gx, gy]).astype(jnp.int32)
    n, m = 32, 8
    west = [(i, (i - 1) % n) for i in range(n)]
    pair_x = [(i, i ^ 1) for i in range(n)]
    odd_x = [(i, (i + (1 if i % 2 else -1)) % n) for i in range(n)]
    pair_y = [(i, i ^ 1) for i in range(m)]
    odd_y = [(i, (i + (1 if i % 2 else -1)) % m) for i in range(m)]

    def swap(x1, od, y1, yo):
        x1 = lax.ppermute(x1, "gx", pair_x)
        od = lax.ppermute(od, "gx", odd_x)
        yo = lax.ppermute(yo, "gy", odd_y)
        y1 = lax.ppermute(y1, "gy", pair_y)
        return x1, od, y1, yo

    moves = jnp.broadcast_to(shift_map[:, None], (16, 256))
    z = jnp.arange(256, dtype=jnp.int32)
    owner = jnp.repeat(image_owner[0], 8)
    target = jnp.broadcast_to((owner * 8 + z % 8)[None], (8, 256))
    source = jnp.broadcast_to(jnp.where(owner == gx, z % 8, -1)[None], (8, 256))

    s_come = lax.ppermute(src_cur, "gx", west)
    r_come = lax.ppermute(rcv_cur, "gx", west)
    come = lax.ppermute(jnp.stack([src_prev, rcv_prev, courant]), "gx", west)
    image_come = lax.ppermute(image, "gx", west)

    (slabs,) = call(scatter_kernel, [sds(256, 256)], [], 1 << 24, moves, target, image)
    for reach in (16, 8, 4, 2, 1):
        if reach > 1:
            pairs = [(i, i + reach) for i in range(0, n, 2 * reach)]
            got = lax.ppermute(slabs[8 * reach :], "gx", pairs)
            slabs = jnp.where(lax.rem(gx, 2 * reach) == 0, slabs[: 8 * reach], got)
        else:
            got = lax.ppermute(slabs[8:], "gx", pair_x)
            slabs = jnp.where(lax.rem(gx, 2) == 0, slabs[:8], got)
    (global_out,) = call(
        gather_kernel, [sds(16, 16, 256)], [], 1 << 22, slabs, source, global_image
    )

    tile = sds(16, 16, 256)
    faces = [sds(2, 4, 16, 256), sds(2, 4, 16, 256), sds(2, 8, 8, 256), sds(2, 8, 8, 256)]
    scratch = [pltpu.VMEM((24, 32, 256), F32)] * 2 + [pltpu.VMEM((16, 16, 256), F32)] * 2
    s, r, *sends = call(
        move_kernel, [tile, tile] + faces, [], 1 << 20, here, moves, src_cur, rcv_cur, s_come, r_come
    )
    for step in range(STEPS):
        halos = swap(*sends)
        ins = [here, s, r, *halos]
        outs = [tile, tile, tile]
        if step == 0:
            ins += [moves, src_prev, rcv_prev, courant, vel_entering, come]
        else:
            ins += [s_old, r_old, velocity, picture]
        if step == STEPS - 1:
            ins += [moves, image, image_come]
        else:
            outs = outs + faces
        if step == 0:
            outs = outs + [tile]
        got = call(functools.partial(step_kernel, step), outs, scratch, 1 << 25, *ins)
        s_old, r_old = s, r
        s, r, picture, *sends = got
        if step == 0:
            velocity = sends.pop()
    return (global_out, picture, s_old, s, r_old, r)


def solution(mesh):
    tiled = P("gx", "gy", None)
    in_specs = (
        tiled,
        P(None, "gy", None),
        tiled,
        tiled,
        tiled,
        tiled,
        tiled,
        tiled,
        P("gy"),
        P("gy", None),
    )
    return jax.shard_map(
        body, mesh=mesh, in_specs=in_specs, out_specs=(tiled,) * 6, check_vma=False
    )
```

```python
import functools

import jax
import jax.numpy as jnp
from jax import lax
from jax.experimental import pallas as pl
from jax.experimental.pallas import tpu as pltpu
from jax.sharding import PartitionSpec as P

STEPS = 4
STENCIL = (-205.0 / 72.0, 8.0 / 5.0, -1.0 / 5.0, 8.0 / 315.0, -1.0 / 560.0)
F32 = jnp.float32
HIGHEST = lax.Precision.HIGHEST
LIMIT = 12 * 1024 * 1024


def sds(*shape):
    return jax.ShapeDtypeStruct(shape, F32)


def call(kernel, outs, scratch, *args, after=()):
    specs = [pl.BlockSpec(memory_space=pl.ANY)] * len(after)
    for a in args:
        space = pltpu.SMEM if a.dtype == jnp.int32 else pltpu.VMEM
        specs.append(pl.BlockSpec(memory_space=space))
    return pl.pallas_call(
        kernel,
        out_shape=outs,
        in_specs=specs,
        out_specs=[pl.BlockSpec(memory_space=pltpu.VMEM)] * len(outs),
        scratch_shapes=scratch,
        compiler_params=pltpu.CompilerParams(vmem_limit_bytes=LIMIT),
        cost_estimate=pl.CostEstimate(flops=1 << 20, bytes_accessed=1 << 20, transcendentals=0),
    )(*after, *args)


def moved_rows(moves):
    row = lax.broadcasted_iota(jnp.int32, (16, 256), 0)
    flags = jnp.zeros((16, 256), jnp.int32)
    for y in range(16):
        flags = jnp.where(row == y, moves[y], flags)
    return flags == 1


def place():
    return lax.axis_index("gx"), lax.axis_index("gy")


def send_faces(fields, sends):
    x1, od, y1, yo = sends
    gx, gy = place()
    even_x, even_y = lax.rem(gx, 2) == 0, lax.rem(gy, 2) == 0
    toward = jnp.where(even_x, 12, 0)
    for f, field in enumerate(fields):
        x1[f] = field[pl.ds(toward, 4)]
        od[f] = field[pl.ds(12 - toward, 4)]
        for half in range(2):
            block = field[8 * half : 8 * half + 8]
            low, high = block[:, 0:4, :], block[:, 12:16, :]
            rows = slice(4 * half, 4 * half + 4)
            y1[f, :, rows, :] = jnp.where(even_y, high, low)
            yo[f, :, rows, :] = jnp.where(even_y, low, high)


def interior_kernel(s, r, s_lap, r_lap, ext_s, ext_r, depth_s, depth_r):
    i = lax.broadcasted_iota(jnp.int32, (256, 256), 0)
    j = lax.broadcasted_iota(jnp.int32, (256, 256), 1)
    apart = jnp.abs(i - j)
    matrix = jnp.where(apart == 0, F32(3.0 * STENCIL[0]), F32(0.0))
    for k in range(1, 5):
        matrix = jnp.where(apart == k, F32(STENCIL[k]), matrix)
    for field, out, ext, depth in ((s, s_lap, ext_s, depth_s), (r, r_lap, ext_r, depth_r)):
        ext[4:20, 8:24, :] = field[...]
        ext[0:4, 8:24, :] = jnp.zeros((4, 16, 256), F32)
        ext[20:24, 8:24, :] = jnp.zeros((4, 16, 256), F32)
        ext[4:20, 0:8, :] = jnp.zeros((16, 8, 256), F32)
        ext[4:20, 24:32, :] = jnp.zeros((16, 8, 256), F32)
        depth[...] = jnp.dot(
            field[...].reshape(256, 256), matrix, precision=HIGHEST, preferred_element_type=F32
        ).reshape(16, 16, 256)
        for x in range(0, 16, 2):
            lap = depth[x : x + 2]
            here, there = slice(4 + x, 6 + x), slice(8, 24)
            for k in range(1, 5):
                pair = ext[4 + x + k : 6 + x + k, there, :] + ext[4 + x - k : 6 + x - k, there, :]
                pair = pair + (ext[here, 8 + k : 24 + k, :] + ext[here, 8 - k : 24 - k, :])
                lap = lap + F32(STENCIL[k]) * pair
            out[x : x + 2] = lap


def face_terms(halos, f):
    x1, od, y1, yo = halos
    gx, gy = place()
    even_x, even_y = lax.rem(gx, 2) == 0, lax.rem(gy, 2) == 0
    zero = F32(0.0)
    a, b = x1[f], od[f]
    low = jnp.where(gx > 0, jnp.where(even_x, b, a), zero)
    high = jnp.where(gx < 31, jnp.where(even_x, a, b), zero)
    planes = [None] * 16
    for p in range(4):
        planes[p] = sum(F32(STENCIL[k]) * low[4 + p - k] for k in range(p + 1, 5))
        planes[12 + p] = sum(F32(STENCIL[k]) * high[p + k - 4] for k in range(4 - p, 5))
    a, b = y1[f], yo[f]
    low = jnp.where(gy > 0, jnp.where(even_y, b, a), zero)
    high = jnp.where(gy < 7, jnp.where(even_y, a, b), zero)
    sub = lax.broadcasted_iota(jnp.int32, (8, 8, 256), 1)
    row = lax.rem(sub, 4)
    low_sum, high_sum = F32(STENCIL[4]) * low, F32(STENCIL[4]) * high
    for k in range(1, 4):
        c = F32(STENCIL[k])
        low_sum = low_sum + jnp.where(row < k, c * pltpu.roll(low, 4 + k, axis=1), zero)
        high_sum = high_sum + jnp.where(row >= 4 - k, c * pltpu.roll(high, 4 - k, axis=1), zero)
    first = sub < 4
    lows = (jnp.where(first, low_sum, zero), jnp.where(first, pltpu.roll(low_sum, 4, axis=1), zero))
    highs = (jnp.where(first, zero, pltpu.roll(high_sum, 4, axis=1)), jnp.where(first, zero, high_sum))
    return planes, lows, highs


def move_kernel(after, moves, s, r, s_in, r_in, s_out, r_out, *sends):
    arrives = place()[0] < 31
    moved = moved_rows(moves)
    for own, come, out in ((s, s_in, s_out), (r, r_in, r_out)):
        for x in range(0, 16, 2):
            out[x : x + 2] = jnp.where(
                moved[None], jnp.where(arrives, come[x : x + 2], F32(0.0)), own[x : x + 2]
            )
    send_faces((s_out, r_out), sends)


def own_kernel(s, r, s_out, r_out):
    s_out[...] = s[...]
    r_out[...] = r[...]


def pack_kernel(after, a, b, c, out):
    out[0] = a[...]
    out[1] = b[...]
    out[2] = c[...]


def update_kernel(step, *refs):
    refs = list(refs)
    take = lambda n: [refs.pop(0) for _ in range(n)]
    last = step == STEPS - 1
    if last:
        take(1)
    s, r, s_lap, r_lap = take(4)
    halos = take(4)
    if step == 0:
        moves, s_prev, r_prev, vel_own, vel_end, come = take(6)
    else:
        s_prev, r_prev, vel, picture = take(4)
    if last:
        moves, image, image_come = take(3)
    else:
        held, got = take(2)
    s_out, r_out, picture_out = take(3)
    if last:
        s_before, r_before = take(2)
    else:
        sends = take(4)
        low, high = take(2)
    if step == 0:
        (vel,) = take(1)

    if step == 0 or last:
        moved = moved_rows(moves)
        arrives = place()[0] < 31
    if last:
        s_before[...] = s[...]
        r_before[...] = r[...]
    if step == 0:
        for x in range(16):
            new = jnp.where(arrives, come[2, x], vel_end[x])
            vel[x] = jnp.where(moved, new, vel_own[x])
    for f, (field, lap, prev, out) in enumerate(
        ((s, s_lap, s_prev, s_out), (r, r_lap, r_prev, r_out))
    ):
        planes, lows, highs = face_terms(halos, f)
        for x in range(16):
            if step == 0:
                old = jnp.where(moved, jnp.where(arrives, come[f, x], F32(0.0)), prev[x])
            else:
                old = prev[x]
            ends = jnp.concatenate([lows[x // 8][x % 8], highs[x // 8][x % 8]], axis=0)
            full = lap[x] + ends
            if planes[x] is not None:
                full = full + planes[x]
            out[x] = 2.0 * field[x] - old + vel[x] * full
    for x in range(16):
        product = s_out[x] * r_out[x]
        if step > 0:
            product = picture[x] + product
        if last:
            product = product + jnp.where(
                moved, jnp.where(arrives, image_come[x], F32(0.0)), image[x]
            )
        picture_out[x] = product
    if not last:
        send_faces((s_out, r_out), sends)
        keep(8 >> step, held, got, low, high)


def distance():
    gx = lax.axis_index("gx")
    return jnp.minimum(gx, 31 - gx)


def keep(reach, held, got, low, high):
    half = 4 * reach
    holds = lax.rem(distance(), 2 * reach) == 0
    low[...] = jnp.where(holds, held[:half], got[:half])
    high[...] = jnp.where(holds, held[half:], got[half:])


def scatter_kernel(after, moves, owner, image, end, low, high):
    upper = lax.axis_index("gx") >= 16
    z = lax.broadcasted_iota(jnp.int32, (8, 256), 1)
    target = jnp.zeros((8, 256), jnp.int32)
    for slab in range(32):
        target = jnp.where(z // 8 == slab, owner[slab], target)
    target = jnp.where(upper, 31 - target, target) * 8 + lax.rem(z, 8)
    rows = lax.broadcasted_iota(jnp.int32, (128, 256), 0)
    pick = jnp.where(rows == target[0:1, :], F32(1.0), F32(0.0))
    tile = jnp.where(upper, end[...], image[...])
    leaving = jnp.where(moved_rows(moves)[None], tile, F32(0.0)).reshape(256, 256)
    slabs = lax.dot_general(
        pick, leaving, (((1,), (1,)), ((), ())), precision=HIGHEST, preferred_element_type=F32
    )
    low[...] = slabs[:64]
    high[...] = slabs[64:]


def gather_kernel(owner, held, got, base, out, token):
    gx = lax.axis_index("gx")
    mine = jnp.int32(0)
    for slab in range(32):
        mine = jnp.where(owner[slab] == gx, slab, mine)
    depth = lax.broadcasted_iota(jnp.int32, (8, 256), 0)
    z = lax.broadcasted_iota(jnp.int32, (8, 256), 1)
    spread = jnp.where(z == 8 * mine + depth, F32(1.0), F32(0.0))
    slab = jnp.where(lax.rem(distance(), 2) == 0, held[...], got[...])
    out[...] = base[...] + lax.dot_general(
        slab, spread, (((0,), (0,)), ((), ())), precision=HIGHEST, preferred_element_type=F32
    ).reshape(16, 16, 256)
    token[...] = jnp.zeros((8, 128), F32)


def body(
    courant,
    vel_entering,
    image,
    src_prev,
    src_cur,
    rcv_prev,
    rcv_cur,
    global_image,
    shift_map,
    image_owner,
):
    n, m = 32, 8
    west = [(i, (i - 1) % n) for i in range(n)]
    pair_x = [(i, i ^ 1) for i in range(n)]
    odd_x = [(i, (i + (1 if i % 2 else -1)) % n) for i in range(n)]
    pair_y = [(i, i ^ 1) for i in range(m)]
    odd_y = [(i, (i + (1 if i % 2 else -1)) % m) for i in range(m)]

    def swap(x1, od, y1, yo):
        x1 = lax.ppermute(x1, "gx", pair_x)
        od = lax.ppermute(od, "gx", odd_x)
        yo = lax.ppermute(yo, "gy", odd_y)
        y1 = lax.ppermute(y1, "gy", pair_y)
        return x1, od, y1, yo

    owner = image_owner.reshape(32)
    tile = sds(16, 16, 256)
    faces = [sds(2, 4, 16, 256), sds(2, 4, 16, 256), sds(2, 8, 8, 256), sds(2, 8, 8, 256)]
    scratch = [pltpu.VMEM((24, 32, 256), F32)] * 2 + [pltpu.VMEM((16, 16, 256), F32)] * 2

    s_come = lax.ppermute(src_cur, "gx", west)
    s_own, r_own = call(own_kernel, [tile, tile], [], src_cur, rcv_cur)
    r_come = lax.ppermute(r_own, "gx", west)
    end = lax.ppermute(image, "gx", [(0, n - 1)])
    s, r, *sends = call(
        move_kernel,
        [tile, tile] + faces,
        [],
        shift_map,
        s_own,
        r_own,
        s_come,
        r_come,
        after=(end,),
    )
    (packed,) = call(pack_kernel, [sds(3, 16, 16, 256)], [], src_prev, rcv_prev, courant, after=(s,))
    come = lax.ppermute(packed, "gx", west)
    image_come = lax.ppermute(image, "gx", west)

    for step in range(STEPS):
        last = step == STEPS - 1
        halos = swap(*sends)
        if step == 0:
            low, high = call(
                scatter_kernel,
                [sds(64, 256)] * 2,
                [],
                shift_map,
                owner,
                image,
                end,
                after=(halos[0],),
            )
        got = lax.ppermute(high, "gx", [(i, i ^ (8 >> step)) for i in range(n)])
        s_lap, r_lap = call(interior_kernel, [tile, tile], scratch, s, r)
        ins = [s, r, s_lap, r_lap, *halos]
        outs, after = [tile] * 3, ()
        if step == 0:
            ins += [shift_map, src_prev, rcv_prev, courant, vel_entering, come]
        else:
            ins += [s_old, r_old, velocity, picture]
        if last:
            global_out, token = call(
                gather_kernel, [tile, sds(8, 128)], [], owner, low, got, global_image
            )
            ins += [shift_map, image, image_come]
            outs, after = outs + [tile] * 2, (token,)
        else:
            ins += [low, got]
            outs = outs + faces + [sds(32 >> step, 256)] * 2
        if step == 0:
            outs = outs + [tile]
        new = call(functools.partial(update_kernel, step), outs, [], *ins, after=after)
        if last:
            s_new, r_new, picture, s, r = new
            return (global_out, picture, s, s_new, r, r_new)
        s_old, r_old = s, r
        s, r, picture, *sends = new
        if step == 0:
            velocity = sends.pop()
        *sends, low, high = sends


def solution(mesh):
    tiled = P("gx", "gy", None)
    in_specs = (
        tiled,
        P(None, "gy", None),
        tiled,
        tiled,
        tiled,
        tiled,
        tiled,
        tiled,
        P("gy"),
        P("gy", None),
    )
    return jax.shard_map(
        body, mesh=mesh, in_specs=in_specs, out_specs=(tiled,) * 6, check_vma=False
    )
```

```python
import functools

import jax
import jax.numpy as jnp
from jax import lax
from jax.experimental import pallas as pl
from jax.experimental.pallas import tpu as pltpu
from jax.sharding import PartitionSpec as P

STEPS = 4
STENCIL = (-205.0 / 72.0, 8.0 / 5.0, -1.0 / 5.0, 8.0 / 315.0, -1.0 / 560.0)
F32 = jnp.float32
HIGHEST = lax.Precision.HIGHEST
LIMIT = 12 * 1024 * 1024


def sds(*shape):
    return jax.ShapeDtypeStruct(shape, F32)


def call(kernel, outs, scratch, *args, after=(), cost=1 << 20):
    specs = [pl.BlockSpec(memory_space=pl.ANY)] * len(after)
    for a in args:
        space = pltpu.SMEM if a.dtype == jnp.int32 else pltpu.VMEM
        specs.append(pl.BlockSpec(memory_space=space))
    return pl.pallas_call(
        kernel,
        out_shape=outs,
        in_specs=specs,
        out_specs=[pl.BlockSpec(memory_space=pltpu.VMEM)] * len(outs),
        scratch_shapes=scratch,
        compiler_params=pltpu.CompilerParams(vmem_limit_bytes=LIMIT),
        cost_estimate=pl.CostEstimate(flops=cost, bytes_accessed=cost, transcendentals=0),
    )(*after, *args)


def place():
    return lax.axis_index("gx"), lax.axis_index("gy")


def send_faces(fields, sends):
    x1, od, y1, yo = sends
    gx, gy = place()
    even_x, even_y = lax.rem(gx, 2) == 0, lax.rem(gy, 2) == 0
    toward = jnp.where(even_x, 12, 0)
    for f, field in enumerate(fields):
        x1[f] = field[pl.ds(toward, 4)]
        od[f] = field[pl.ds(12 - toward, 4)]
        for half in range(2):
            block = field[8 * half : 8 * half + 8]
            low, high = block[:, 0:4, :], block[:, 12:16, :]
            rows = slice(4 * half, 4 * half + 4)
            y1[f, :, rows, :] = jnp.where(even_y, high, low)
            yo[f, :, rows, :] = jnp.where(even_y, low, high)


def interior_kernel(s, r, s_lap, r_lap, ext_s, ext_r, depth_s, depth_r):
    i = lax.broadcasted_iota(jnp.int32, (256, 256), 0)
    j = lax.broadcasted_iota(jnp.int32, (256, 256), 1)
    apart = jnp.abs(i - j)
    matrix = jnp.where(apart == 0, F32(3.0 * STENCIL[0]), F32(0.0))
    for k in range(1, 5):
        matrix = jnp.where(apart == k, F32(STENCIL[k]), matrix)
    for field, out, ext, depth in ((s, s_lap, ext_s, depth_s), (r, r_lap, ext_r, depth_r)):
        ext[4:20, 8:24, :] = field[...]
        ext[0:4, 8:24, :] = jnp.zeros((4, 16, 256), F32)
        ext[20:24, 8:24, :] = jnp.zeros((4, 16, 256), F32)
        ext[4:20, 0:8, :] = jnp.zeros((16, 8, 256), F32)
        ext[4:20, 24:32, :] = jnp.zeros((16, 8, 256), F32)
        depth[...] = jnp.dot(
            field[...].reshape(256, 256), matrix, precision=HIGHEST, preferred_element_type=F32
        ).reshape(16, 16, 256)
        for x in range(0, 16, 2):
            lap = depth[x : x + 2]
            here, there = slice(4 + x, 6 + x), slice(8, 24)
            for k in range(1, 5):
                pair = ext[4 + x + k : 6 + x + k, there, :] + ext[4 + x - k : 6 + x - k, there, :]
                pair = pair + (ext[here, 8 + k : 24 + k, :] + ext[here, 8 - k : 24 - k, :])
                lap = lap + F32(STENCIL[k]) * pair
            out[x : x + 2] = lap


def face_terms(halos, f):
    x1, od, y1, yo = halos
    gx, gy = place()
    even_x, even_y = lax.rem(gx, 2) == 0, lax.rem(gy, 2) == 0
    zero = F32(0.0)
    a, b = x1[f], od[f]
    low = jnp.where(gx > 0, jnp.where(even_x, b, a), zero)
    high = jnp.where(gx < 31, jnp.where(even_x, a, b), zero)
    planes = [None] * 16
    for p in range(4):
        planes[p] = sum(F32(STENCIL[k]) * low[4 + p - k] for k in range(p + 1, 5))
        planes[12 + p] = sum(F32(STENCIL[k]) * high[p + k - 4] for k in range(4 - p, 5))
    a, b = y1[f], yo[f]
    low = jnp.where(gy > 0, jnp.where(even_y, b, a), zero)
    high = jnp.where(gy < 7, jnp.where(even_y, a, b), zero)
    sub = lax.broadcasted_iota(jnp.int32, (8, 8, 256), 1)
    row = lax.rem(sub, 4)
    low_sum, high_sum = F32(STENCIL[4]) * low, F32(STENCIL[4]) * high
    for k in range(1, 4):
        c = F32(STENCIL[k])
        low_sum = low_sum + jnp.where(row < k, c * pltpu.roll(low, 4 + k, axis=1), zero)
        high_sum = high_sum + jnp.where(row >= 4 - k, c * pltpu.roll(high, 4 - k, axis=1), zero)
    first = sub < 4
    lows = (jnp.where(first, low_sum, zero), jnp.where(first, pltpu.roll(low_sum, 4, axis=1), zero))
    highs = (jnp.where(first, zero, pltpu.roll(high_sum, 4, axis=1)), jnp.where(first, zero, high_sum))
    return planes, lows, highs


def move_kernel(moves, s, r, s_in, r_in, s_out, r_out, *sends):
    arrives = place()[0] < 31
    moved = (moves[...] == 1.0)
    for own, come, out in ((s, s_in, s_out), (r, r_in, r_out)):
        for x in range(0, 16, 2):
            out[x : x + 2] = jnp.where(
                moved[None], jnp.where(arrives, come[x : x + 2], F32(0.0)), own[x : x + 2]
            )
    send_faces((s_out, r_out), sends)


def own_kernel(moves, s, r, s_out, r_out, mask):
    s_out[...] = s[...]
    r_out[...] = r[...]
    row = lax.broadcasted_iota(jnp.int32, (16, 256), 0)
    flags = jnp.zeros((16, 256), jnp.int32)
    for y in range(16):
        flags = jnp.where(row == y, moves[y], flags)
    mask[...] = jnp.where(flags == 1, F32(1.0), F32(0.0))


def first_kernel(vel, image, out):
    out[...] = jnp.where(place()[0] == 0, image[...], vel[...])


def copy_kernel(after, a, out):
    out[...] = a[...]


def update_kernel(step, *refs):
    refs = list(refs)
    take = lambda n: [refs.pop(0) for _ in range(n)]
    last = step == STEPS - 1
    if last:
        take(1)
    s, r, s_lap, r_lap = take(4)
    halos = take(4)
    if step == 0:
        moves, s_prev, r_prev, vel_own, vel_end, s_come, r_come, vel_come = take(8)
    else:
        s_prev, r_prev, vel, picture = take(4)
    if last:
        moves, image, image_come = take(3)
    s_out, r_out, picture_out = take(3)
    if last:
        s_before, r_before = take(2)
    else:
        sends = take(4)
    if step == 0:
        (vel,) = take(1)

    if step == 0 or last:
        moved = (moves[...] == 1.0)
        arrives = place()[0] < 31
    if last:
        s_before[...] = s[...]
        r_before[...] = r[...]
    if step == 0:
        for x in range(16):
            new = jnp.where(arrives, vel_come[x], vel_end[x])
            vel[x] = jnp.where(moved, new, vel_own[x])
    if step > 0:
        s_come = r_come = None
    for f, (field, lap, prev, come, out) in enumerate(
        ((s, s_lap, s_prev, s_come, s_out), (r, r_lap, r_prev, r_come, r_out))
    ):
        planes, lows, highs = face_terms(halos, f)
        for x in range(16):
            if step == 0:
                old = jnp.where(moved, jnp.where(arrives, come[x], F32(0.0)), prev[x])
            else:
                old = prev[x]
            ends = jnp.concatenate([lows[x // 8][x % 8], highs[x // 8][x % 8]], axis=0)
            full = lap[x] + ends
            if planes[x] is not None:
                full = full + planes[x]
            out[x] = 2.0 * field[x] - old + vel[x] * full
    for x in range(16):
        product = s_out[x] * r_out[x]
        if step > 0:
            product = picture[x] + product
        if last:
            product = product + jnp.where(
                moved, jnp.where(arrives, image_come[x], F32(0.0)), image[x]
            )
        picture_out[x] = product
    if not last:
        send_faces((s_out, r_out), sends)


def distance():
    gx = lax.axis_index("gx")
    return jnp.minimum(gx, 31 - gx)


def keep_kernel(reach, after, held, got, low, high):
    half = 4 * reach
    holds = lax.rem(distance(), 2 * reach) == 0
    low[...] = jnp.where(holds, held[:half], got[:half])
    high[...] = jnp.where(holds, held[half:], got[half:])


def scatter_kernel(after, moves, owner, image, come, low, high):
    upper = lax.axis_index("gx") >= 16
    z = lax.broadcasted_iota(jnp.int32, (8, 256), 1)
    target = jnp.zeros((8, 256), jnp.int32)
    for slab in range(32):
        target = jnp.where(z // 8 == slab, owner[slab], target)
    target = jnp.where(upper, 31 - target, target) * 8 + lax.rem(z, 8)
    rows = lax.broadcasted_iota(jnp.int32, (128, 256), 0)
    pick = jnp.where(rows == target[0:1, :], F32(1.0), F32(0.0))
    tile = jnp.where(upper, come[...], image[...])
    leaving = jnp.where((moves[...] == 1.0)[None], tile, F32(0.0)).reshape(256, 256)
    slabs = lax.dot_general(
        pick, leaving, (((1,), (1,)), ((), ())), precision=HIGHEST, preferred_element_type=F32
    )
    low[...] = slabs[:64]
    high[...] = slabs[64:]


def gather_kernel(owner, held, got, base, out, token):
    gx = lax.axis_index("gx")
    mine = jnp.int32(0)
    for slab in range(32):
        mine = jnp.where(owner[slab] == gx, slab, mine)
    depth = lax.broadcasted_iota(jnp.int32, (8, 256), 0)
    z = lax.broadcasted_iota(jnp.int32, (8, 256), 1)
    spread = jnp.where(z == 8 * mine + depth, F32(1.0), F32(0.0))
    slab = jnp.where(lax.rem(distance(), 2) == 0, held[...], got[...])
    out[...] = base[...] + lax.dot_general(
        slab, spread, (((0,), (0,)), ((), ())), precision=HIGHEST, preferred_element_type=F32
    ).reshape(16, 16, 256)
    token[...] = jnp.zeros((8, 128), F32)


def body(
    courant,
    vel_entering,
    image,
    src_prev,
    src_cur,
    rcv_prev,
    rcv_cur,
    global_image,
    shift_map,
    image_owner,
):
    n, m = 32, 8
    west = [(i, (i - 1) % n) for i in range(n)]
    pair_x = [(i, i ^ 1) for i in range(n)]
    odd_x = [(i, (i + (1 if i % 2 else -1)) % n) for i in range(n)]
    pair_y = [(i, i ^ 1) for i in range(m)]
    odd_y = [(i, (i + (1 if i % 2 else -1)) % m) for i in range(m)]

    def swap(x1, od, y1, yo):
        x1 = lax.ppermute(x1, "gx", pair_x)
        od = lax.ppermute(od, "gx", odd_x)
        yo = lax.ppermute(yo, "gy", odd_y)
        y1 = lax.ppermute(y1, "gy", pair_y)
        return x1, od, y1, yo

    owner = image_owner.reshape(32)
    tile = sds(16, 16, 256)
    faces = [sds(2, 4, 16, 256), sds(2, 4, 16, 256), sds(2, 8, 8, 256), sds(2, 8, 8, 256)]
    scratch = [pltpu.VMEM((24, 32, 256), F32)] * 2 + [pltpu.VMEM((16, 16, 256), F32)] * 2

    s_come = lax.ppermute(src_cur, "gx", west)
    r_come = lax.ppermute(rcv_cur, "gx", west)
    sp_come = lax.ppermute(src_prev, "gx", west)
    rp_come = lax.ppermute(rcv_prev, "gx", west)
    (vel_send,) = call(first_kernel, [tile], [], courant, image)
    vel_come = lax.ppermute(vel_send, "gx", west)
    s_own, r_own, mask = call(
        own_kernel, [tile] * 2 + [sds(16, 256)], [], shift_map, src_cur, rcv_cur
    )
    s, r, *sends = call(
        move_kernel, [tile, tile] + faces, [], mask, s_own, r_own, s_come, r_come
    )

    for step in range(STEPS):
        last = step == STEPS - 1
        halos = swap(*sends)
        if step == 0:
            low, high = call(
                scatter_kernel,
                [sds(64, 256)] * 2,
                [],
                mask,
                owner,
                image,
                vel_come,
                after=(halos[0],),
            )
        else:
            low, high = call(
                functools.partial(keep_kernel, 16 >> step),
                [sds(64 >> step, 256)] * 2,
                [],
                low,
                got,
                after=(halos[0],),
            )
        got = lax.ppermute(high, "gx", [(i, i ^ (8 >> step)) for i in range(n)])
        if step == 1:
            (image_send,) = call(copy_kernel, [tile], [], image, after=(halos[1],))
            image_come = lax.ppermute(image_send, "gx", west)
        s_lap, r_lap = call(interior_kernel, [tile, tile], scratch, s, r)
        ins = [s, r, s_lap, r_lap, *halos]
        outs, after = [tile] * 3, ()
        if step == 0:
            ins += [mask, src_prev, rcv_prev, courant, vel_entering]
            ins += [sp_come, rp_come, vel_come]
        else:
            ins += [s_old, r_old, velocity, picture]
        if last:
            global_out, token = call(
                gather_kernel, [tile, sds(8, 128)], [], owner, low, got, global_image
            )
            ins += [mask, image, image_come]
            outs, after = outs + [tile] * 2, (token,)
        else:
            outs = outs + faces
        if step == 0:
            outs = outs + [tile]
        new = call(functools.partial(update_kernel, step), outs, [], *ins, after=after)
        if last:
            s_new, r_new, picture, s, r = new
            return (global_out, picture, s, s_new, r, r_new)
        s_old, r_old = s, r
        s, r, picture, *sends = new
        if step == 0:
            velocity = sends.pop()


def solution(mesh):
    tiled = P("gx", "gy", None)
    in_specs = (
        tiled,
        P(None, "gy", None),
        tiled,
        tiled,
        tiled,
        tiled,
        tiled,
        tiled,
        P("gy"),
        P("gy", None),
    )
    return jax.shard_map(
        body, mesh=mesh, in_specs=in_specs, out_specs=(tiled,) * 6, check_vma=False
    )
```

```python
import functools

import jax
import jax.numpy as jnp
from jax import lax
from jax.experimental import pallas as pl
from jax.experimental.pallas import tpu as pltpu
from jax.sharding import PartitionSpec as P

STEPS = 4
STENCIL = (-205.0 / 72.0, 8.0 / 5.0, -1.0 / 5.0, 8.0 / 315.0, -1.0 / 560.0)
F32 = jnp.float32
HIGHEST = lax.Precision.HIGHEST
LIMIT = 12 * 1024 * 1024
WAITS = (1, 0, 0, 1)


def sds(*shape):
    return jax.ShapeDtypeStruct(shape, F32)


def call(kernel, outs, scratch, *args, after=(), cost=1 << 20):
    specs = [pl.BlockSpec(memory_space=pl.ANY)] * len(after)
    for a in args:
        space = pltpu.SMEM if a.dtype == jnp.int32 else pltpu.VMEM
        specs.append(pl.BlockSpec(memory_space=space))
    return pl.pallas_call(
        kernel,
        out_shape=outs,
        in_specs=specs,
        out_specs=[pl.BlockSpec(memory_space=pltpu.VMEM)] * len(outs),
        scratch_shapes=scratch,
        compiler_params=pltpu.CompilerParams(vmem_limit_bytes=LIMIT),
        cost_estimate=pl.CostEstimate(flops=cost, bytes_accessed=cost, transcendentals=0),
    )(*after, *args)


def place():
    return lax.axis_index("gx"), lax.axis_index("gy")


def send_faces(fields, sends):
    x1, od, y1, yo = sends
    gx, gy = place()
    even_x, even_y = lax.rem(gx, 2) == 0, lax.rem(gy, 2) == 0
    toward = jnp.where(even_x, 12, 0)
    for f, field in enumerate(fields):
        x1[f] = field[pl.ds(toward, 4)]
        od[f] = field[pl.ds(12 - toward, 4)]
        for half in range(2):
            block = field[8 * half : 8 * half + 8]
            low, high = block[:, 0:4, :], block[:, 12:16, :]
            rows = slice(4 * half, 4 * half + 4)
            y1[f, :, rows, :] = jnp.where(even_y, high, low)
            yo[f, :, rows, :] = jnp.where(even_y, low, high)


def interior_kernel(s, r, s_lap, r_lap, ext_s, ext_r, depth_s, depth_r):
    i = lax.broadcasted_iota(jnp.int32, (256, 256), 0)
    j = lax.broadcasted_iota(jnp.int32, (256, 256), 1)
    apart = jnp.abs(i - j)
    matrix = jnp.where(apart == 0, F32(3.0 * STENCIL[0]), F32(0.0))
    for k in range(1, 5):
        matrix = jnp.where(apart == k, F32(STENCIL[k]), matrix)
    for field, out, ext, depth in ((s, s_lap, ext_s, depth_s), (r, r_lap, ext_r, depth_r)):
        ext[4:20, 8:24, :] = field[...]
        ext[0:4, 8:24, :] = jnp.zeros((4, 16, 256), F32)
        ext[20:24, 8:24, :] = jnp.zeros((4, 16, 256), F32)
        ext[4:20, 0:8, :] = jnp.zeros((16, 8, 256), F32)
        ext[4:20, 24:32, :] = jnp.zeros((16, 8, 256), F32)
        depth[...] = jnp.dot(
            field[...].reshape(256, 256), matrix, precision=HIGHEST, preferred_element_type=F32
        ).reshape(16, 16, 256)
        for x in range(0, 16, 2):
            lap = depth[x : x + 2]
            here, there = slice(4 + x, 6 + x), slice(8, 24)
            for k in range(1, 5):
                pair = ext[4 + x + k : 6 + x + k, there, :] + ext[4 + x - k : 6 + x - k, there, :]
                pair = pair + (ext[here, 8 + k : 24 + k, :] + ext[here, 8 - k : 24 - k, :])
                lap = lap + F32(STENCIL[k]) * pair
            out[x : x + 2] = lap


def face_terms(halos, f):
    x1, od, y1, yo = halos
    gx, gy = place()
    even_x, even_y = lax.rem(gx, 2) == 0, lax.rem(gy, 2) == 0
    zero = F32(0.0)
    a, b = x1[f], od[f]
    low = jnp.where(gx > 0, jnp.where(even_x, b, a), zero)
    high = jnp.where(gx < 31, jnp.where(even_x, a, b), zero)
    planes = [None] * 16
    for p in range(4):
        planes[p] = sum(F32(STENCIL[k]) * low[4 + p - k] for k in range(p + 1, 5))
        planes[12 + p] = sum(F32(STENCIL[k]) * high[p + k - 4] for k in range(4 - p, 5))
    a, b = y1[f], yo[f]
    low = jnp.where(gy > 0, jnp.where(even_y, b, a), zero)
    high = jnp.where(gy < 7, jnp.where(even_y, a, b), zero)
    sub = lax.broadcasted_iota(jnp.int32, (8, 8, 256), 1)
    row = lax.rem(sub, 4)
    low_sum, high_sum = F32(STENCIL[4]) * low, F32(STENCIL[4]) * high
    for k in range(1, 4):
        c = F32(STENCIL[k])
        low_sum = low_sum + jnp.where(row < k, c * pltpu.roll(low, 4 + k, axis=1), zero)
        high_sum = high_sum + jnp.where(row >= 4 - k, c * pltpu.roll(high, 4 - k, axis=1), zero)
    first = sub < 4
    lows = (jnp.where(first, low_sum, zero), jnp.where(first, pltpu.roll(low_sum, 4, axis=1), zero))
    highs = (jnp.where(first, zero, pltpu.roll(high_sum, 4, axis=1)), jnp.where(first, zero, high_sum))
    return planes, lows, highs


def move_kernel(moves, s, r, s_in, r_in, s_out, r_out, *sends):
    arrives = place()[0] < 31
    moved = (moves[...] == 1.0)
    for own, come, out in ((s, s_in, s_out), (r, r_in, r_out)):
        for x in range(0, 16, 2):
            out[x : x + 2] = jnp.where(
                moved[None], jnp.where(arrives, come[x : x + 2], F32(0.0)), own[x : x + 2]
            )
    send_faces((s_out, r_out), sends)


def own_kernel(moves, s, r, s_out, r_out, mask):
    s_out[...] = s[...]
    r_out[...] = r[...]
    row = lax.broadcasted_iota(jnp.int32, (16, 256), 0)
    flags = jnp.zeros((16, 256), jnp.int32)
    for y in range(16):
        flags = jnp.where(row == y, moves[y], flags)
    mask[...] = jnp.where(flags == 1, F32(1.0), F32(0.0))


def first_kernel(vel, image, out):
    out[...] = jnp.where(place()[0] == 0, image[...], vel[...])


def copy_kernel(after, a, out):
    out[...] = a[...]


def update_kernel(step, *refs):
    refs = list(refs)
    take = lambda n: [refs.pop(0) for _ in range(n)]
    last = step == STEPS - 1
    take(WAITS[step])
    s, r, s_lap, r_lap = take(4)
    halos = take(4)
    if step == 0:
        moves, s_prev, r_prev, vel_own, vel_end, s_come, r_come, vel_come = take(8)
    else:
        s_prev, r_prev, vel, picture = take(4)
    if last:
        moves, image, image_come = take(3)
    s_out, r_out, picture_out = take(3)
    if last:
        s_before, r_before = take(2)
    else:
        sends = take(4)
    if step == 0:
        (vel,) = take(1)

    if step == 0 or last:
        moved = (moves[...] == 1.0)
        arrives = place()[0] < 31
    if last:
        s_before[...] = s[...]
        r_before[...] = r[...]
    if step == 0:
        for x in range(16):
            new = jnp.where(arrives, vel_come[x], vel_end[x])
            vel[x] = jnp.where(moved, new, vel_own[x])
    if step > 0:
        s_come = r_come = None
    for f, (field, lap, prev, come, out) in enumerate(
        ((s, s_lap, s_prev, s_come, s_out), (r, r_lap, r_prev, r_come, r_out))
    ):
        planes, lows, highs = face_terms(halos, f)
        for x in range(16):
            if step == 0:
                old = jnp.where(moved, jnp.where(arrives, come[x], F32(0.0)), prev[x])
            else:
                old = prev[x]
            ends = jnp.concatenate([lows[x // 8][x % 8], highs[x // 8][x % 8]], axis=0)
            full = lap[x] + ends
            if planes[x] is not None:
                full = full + planes[x]
            out[x] = 2.0 * field[x] - old + vel[x] * full
    for x in range(16):
        product = s_out[x] * r_out[x]
        if step > 0:
            product = picture[x] + product
        if last:
            product = product + jnp.where(
                moved, jnp.where(arrives, image_come[x], F32(0.0)), image[x]
            )
        picture_out[x] = product
    if not last:
        send_faces((s_out, r_out), sends)


def distance():
    gx = lax.axis_index("gx")
    return jnp.minimum(gx, 31 - gx)


def keep_kernel(reach, after, held, got, low, high):
    half = 4 * reach
    holds = lax.rem(distance(), 2 * reach) == 0
    low[...] = jnp.where(holds, held[:half], got[:half])
    high[...] = jnp.where(holds, held[half:], got[half:])


def scatter_kernel(after, moves, owner, image, come, low, high):
    upper = lax.axis_index("gx") >= 16
    z = lax.broadcasted_iota(jnp.int32, (8, 256), 1)
    target = jnp.zeros((8, 256), jnp.int32)
    for slab in range(32):
        target = jnp.where(z // 8 == slab, owner[slab], target)
    target = jnp.where(upper, 31 - target, target) * 8 + lax.rem(z, 8)
    rows = lax.broadcasted_iota(jnp.int32, (128, 256), 0)
    pick = jnp.where(rows == target[0:1, :], F32(1.0), F32(0.0))
    tile = jnp.where(upper, come[...], image[...])
    leaving = jnp.where((moves[...] == 1.0)[None], tile, F32(0.0)).reshape(256, 256)
    slabs = lax.dot_general(
        pick, leaving, (((1,), (1,)), ((), ())), precision=HIGHEST, preferred_element_type=F32
    )
    low[...] = slabs[:64]
    high[...] = slabs[64:]


def gather_kernel(owner, held, got, base, out, token):
    gx = lax.axis_index("gx")
    mine = jnp.int32(0)
    for slab in range(32):
        mine = jnp.where(owner[slab] == gx, slab, mine)
    depth = lax.broadcasted_iota(jnp.int32, (8, 256), 0)
    z = lax.broadcasted_iota(jnp.int32, (8, 256), 1)
    spread = jnp.where(z == 8 * mine + depth, F32(1.0), F32(0.0))
    slab = jnp.where(lax.rem(distance(), 2) == 0, held[...], got[...])
    out[...] = base[...] + lax.dot_general(
        slab, spread, (((0,), (0,)), ((), ())), precision=HIGHEST, preferred_element_type=F32
    ).reshape(16, 16, 256)
    token[...] = jnp.zeros((8, 128), F32)


def body(
    courant,
    vel_entering,
    image,
    src_prev,
    src_cur,
    rcv_prev,
    rcv_cur,
    global_image,
    shift_map,
    image_owner,
):
    n, m = 32, 8
    west = [(i, (i - 1) % n) for i in range(n)]
    pair_x = [(i, i ^ 1) for i in range(n)]
    odd_x = [(i, (i + (1 if i % 2 else -1)) % n) for i in range(n)]
    pair_y = [(i, i ^ 1) for i in range(m)]
    odd_y = [(i, (i + (1 if i % 2 else -1)) % m) for i in range(m)]

    def swap(x1, od, y1, yo):
        x1 = lax.ppermute(x1, "gx", pair_x)
        od = lax.ppermute(od, "gx", odd_x)
        yo = lax.ppermute(yo, "gy", odd_y)
        y1 = lax.ppermute(y1, "gy", pair_y)
        return x1, od, y1, yo

    owner = image_owner.reshape(32)
    tile = sds(16, 16, 256)
    faces = [sds(2, 4, 16, 256), sds(2, 4, 16, 256), sds(2, 8, 8, 256), sds(2, 8, 8, 256)]
    scratch = [pltpu.VMEM((24, 32, 256), F32)] * 2 + [pltpu.VMEM((16, 16, 256), F32)] * 2

    s_come = lax.ppermute(src_cur, "gx", west)
    r_come = lax.ppermute(rcv_cur, "gx", west)
    sp_come = lax.ppermute(src_prev, "gx", west)
    rp_come = lax.ppermute(rcv_prev, "gx", west)
    (vel_send,) = call(first_kernel, [tile], [], courant, image)
    vel_come = lax.ppermute(vel_send, "gx", west)
    s_own, r_own, mask = call(
        own_kernel, [tile] * 2 + [sds(16, 256)], [], shift_map, src_cur, rcv_cur
    )
    s, r, *sends = call(
        move_kernel, [tile, tile] + faces, [], mask, s_own, r_own, s_come, r_come
    )

    for step in range(STEPS):
        last = step == STEPS - 1
        halos = swap(*sends)
        if step == 0:
            low, high = call(
                scatter_kernel,
                [sds(64, 256)] * 2,
                [],
                mask,
                owner,
                image,
                vel_come,
                after=(halos[0],),
            )
        else:
            low, high = call(
                functools.partial(keep_kernel, 16 >> step),
                [sds(64 >> step, 256)] * 2,
                [],
                low,
                got,
                after=(halos[0],),
            )
        got = lax.ppermute(high, "gx", [(i, i ^ (8 >> step)) for i in range(n)])
        if step == 1:
            (image_send,) = call(copy_kernel, [tile], [], image, after=(halos[1],))
            image_come = lax.ppermute(image_send, "gx", west)
        s_lap, r_lap = call(interior_kernel, [tile, tile], scratch, s, r)
        ins = [s, r, s_lap, r_lap, *halos]
        outs = [tile] * 3
        if step == 0:
            ins += [mask, src_prev, rcv_prev, courant, vel_entering]
            ins += [sp_come, rp_come, vel_come]
        else:
            ins += [s_old, r_old, velocity, picture]
        if last:
            global_out, token = call(
                gather_kernel, [tile, sds(8, 128)], [], owner, low, got, global_image
            )
            ins += [mask, image, image_come]
            outs = outs + [tile] * 2
        else:
            outs = outs + faces
        if step == 0:
            outs = outs + [tile]
        after = ()
        if step == 0:
            after = (got,)
        if step == 3:
            after = (token,)
        new = call(functools.partial(update_kernel, step), outs, [], *ins, after=after)
        if last:
            s_new, r_new, picture, s, r = new
            return (global_out, picture, s, s_new, r, r_new)
        s_old, r_old = s, r
        s, r, picture, *sends = new
        if step == 0:
            velocity = sends.pop()


def solution(mesh):
    tiled = P("gx", "gy", None)
    in_specs = (
        tiled,
        P(None, "gy", None),
        tiled,
        tiled,
        tiled,
        tiled,
        tiled,
        tiled,
        P("gy"),
        P("gy", None),
    )
    return jax.shard_map(
        body, mesh=mesh, in_specs=in_specs, out_specs=(tiled,) * 6, check_vma=False
    )
```

```python
import functools

import jax
import jax.numpy as jnp
from jax import lax
from jax.experimental import pallas as pl
from jax.experimental.pallas import tpu as pltpu
from jax.sharding import PartitionSpec as P

STEPS = 4
STENCIL = (-205.0 / 72.0, 8.0 / 5.0, -1.0 / 5.0, 8.0 / 315.0, -1.0 / 560.0)
F32 = jnp.float32
HIGHEST = lax.Precision.HIGHEST
LIMIT = 12 * 1024 * 1024
WAITS = (1, 0, 0, 1)


def sds(*shape):
    return jax.ShapeDtypeStruct(shape, F32)


def call(kernel, outs, scratch, *args, after=(), cost=1 << 20):
    specs = [pl.BlockSpec(memory_space=pl.ANY)] * len(after)
    for a in args:
        space = pltpu.SMEM if a.dtype == jnp.int32 else pltpu.VMEM
        specs.append(pl.BlockSpec(memory_space=space))
    return pl.pallas_call(
        kernel,
        out_shape=outs,
        in_specs=specs,
        out_specs=[pl.BlockSpec(memory_space=pltpu.VMEM)] * len(outs),
        scratch_shapes=scratch,
        compiler_params=pltpu.CompilerParams(vmem_limit_bytes=LIMIT),
        cost_estimate=pl.CostEstimate(flops=cost, bytes_accessed=cost, transcendentals=0),
    )(*after, *args)


def place():
    return lax.axis_index("gx"), lax.axis_index("gy")


def send_faces(fields, sends):
    x1, od, y1, yo = sends
    gx, gy = place()
    even_x, even_y = lax.rem(gx, 2) == 0, lax.rem(gy, 2) == 0
    toward = jnp.where(even_x, 12, 0)
    for f, field in enumerate(fields):
        x1[f] = field[pl.ds(toward, 4)]
        od[f] = field[pl.ds(12 - toward, 4)]
        for half in range(2):
            block = field[8 * half : 8 * half + 8]
            low, high = block[:, 0:4, :], block[:, 12:16, :]
            rows = slice(4 * half, 4 * half + 4)
            y1[f, :, rows, :] = jnp.where(even_y, high, low)
            yo[f, :, rows, :] = jnp.where(even_y, low, high)


def interior_kernel(s, r, s_lap, r_lap, ext_s, ext_r, depth_s, depth_r):
    i = lax.broadcasted_iota(jnp.int32, (256, 256), 0)
    j = lax.broadcasted_iota(jnp.int32, (256, 256), 1)
    apart = jnp.abs(i - j)
    matrix = jnp.where(apart == 0, F32(3.0 * STENCIL[0]), F32(0.0))
    for k in range(1, 5):
        matrix = jnp.where(apart == k, F32(STENCIL[k]), matrix)
    for field, out, ext, depth in ((s, s_lap, ext_s, depth_s), (r, r_lap, ext_r, depth_r)):
        ext[4:20, 8:24, :] = field[...]
        ext[0:4, 8:24, :] = jnp.zeros((4, 16, 256), F32)
        ext[20:24, 8:24, :] = jnp.zeros((4, 16, 256), F32)
        ext[4:20, 0:8, :] = jnp.zeros((16, 8, 256), F32)
        ext[4:20, 24:32, :] = jnp.zeros((16, 8, 256), F32)
        depth[...] = jnp.dot(
            field[...].reshape(256, 256), matrix, precision=HIGHEST, preferred_element_type=F32
        ).reshape(16, 16, 256)
        for x in range(0, 16, 2):
            lap = depth[x : x + 2]
            here, there = slice(4 + x, 6 + x), slice(8, 24)
            for k in range(1, 5):
                pair = ext[4 + x + k : 6 + x + k, there, :] + ext[4 + x - k : 6 + x - k, there, :]
                pair = pair + (ext[here, 8 + k : 24 + k, :] + ext[here, 8 - k : 24 - k, :])
                lap = lap + F32(STENCIL[k]) * pair
            out[x : x + 2] = lap


def face_terms(halos, f):
    x1, od, y1, yo = halos
    gx, gy = place()
    even_x, even_y = lax.rem(gx, 2) == 0, lax.rem(gy, 2) == 0
    zero = F32(0.0)
    a, b = x1[f], od[f]
    low = jnp.where(gx > 0, jnp.where(even_x, b, a), zero)
    high = jnp.where(gx < 31, jnp.where(even_x, a, b), zero)
    planes = [None] * 16
    for p in range(4):
        planes[p] = sum(F32(STENCIL[k]) * low[4 + p - k] for k in range(p + 1, 5))
        planes[12 + p] = sum(F32(STENCIL[k]) * high[p + k - 4] for k in range(4 - p, 5))
    a, b = y1[f], yo[f]
    low = jnp.where(gy > 0, jnp.where(even_y, b, a), zero)
    high = jnp.where(gy < 7, jnp.where(even_y, a, b), zero)
    sub = lax.broadcasted_iota(jnp.int32, (8, 8, 256), 1)
    row = lax.rem(sub, 4)
    low_sum, high_sum = F32(STENCIL[4]) * low, F32(STENCIL[4]) * high
    for k in range(1, 4):
        c = F32(STENCIL[k])
        low_sum = low_sum + jnp.where(row < k, c * pltpu.roll(low, 4 + k, axis=1), zero)
        high_sum = high_sum + jnp.where(row >= 4 - k, c * pltpu.roll(high, 4 - k, axis=1), zero)
    first = sub < 4
    lows = (jnp.where(first, low_sum, zero), jnp.where(first, pltpu.roll(low_sum, 4, axis=1), zero))
    highs = (jnp.where(first, zero, pltpu.roll(high_sum, 4, axis=1)), jnp.where(first, zero, high_sum))
    return planes, lows, highs


def move_kernel(moves, s, r, s_in, r_in, s_out, r_out, *sends):
    arrives = place()[0] < 31
    moved = (moves[...] == 1.0)
    for own, come, out in ((s, s_in, s_out), (r, r_in, r_out)):
        for x in range(0, 16, 2):
            out[x : x + 2] = jnp.where(
                moved[None], jnp.where(arrives, come[x : x + 2], F32(0.0)), own[x : x + 2]
            )
    send_faces((s_out, r_out), sends)


def own_kernel(moves, s, r, s_out, r_out, mask):
    s_out[...] = s[...]
    r_out[...] = r[...]
    row = lax.broadcasted_iota(jnp.int32, (16, 256), 0)
    flags = jnp.zeros((16, 256), jnp.int32)
    for y in range(16):
        flags = jnp.where(row == y, moves[y], flags)
    mask[...] = jnp.where(flags == 1, F32(1.0), F32(0.0))


def first_kernel(vel, image, out):
    out[...] = jnp.where(place()[0] == 0, image[...], vel[...])


def copy_kernel(after, a, out):
    out[...] = a[...]


def update_kernel(step, *refs):
    refs = list(refs)
    take = lambda n: [refs.pop(0) for _ in range(n)]
    last = step == STEPS - 1
    take(WAITS[step])
    s, r, s_lap, r_lap = take(4)
    halos = take(4)
    if step == 0:
        moves, s_prev, r_prev, vel_own, vel_end, s_come, r_come, vel_come = take(8)
    else:
        s_prev, r_prev, vel, picture = take(4)
    if last:
        moves, image, image_come = take(3)
    s_out, r_out, picture_out = take(3)
    if last:
        s_before, r_before = take(2)
    else:
        sends = take(4)
    if step == 0:
        (vel,) = take(1)

    if step == 0 or last:
        moved = (moves[...] == 1.0)
        arrives = place()[0] < 31
    if last:
        s_before[...] = s[...]
        r_before[...] = r[...]
    if step == 0:
        for x in range(16):
            new = jnp.where(arrives, vel_come[x], vel_end[x])
            vel[x] = jnp.where(moved, new, vel_own[x])
    if step > 0:
        s_come = r_come = None
    for f, (field, lap, prev, come, out) in enumerate(
        ((s, s_lap, s_prev, s_come, s_out), (r, r_lap, r_prev, r_come, r_out))
    ):
        planes, lows, highs = face_terms(halos, f)
        for x in range(16):
            if step == 0:
                old = jnp.where(moved, jnp.where(arrives, come[x], F32(0.0)), prev[x])
            else:
                old = prev[x]
            ends = jnp.concatenate([lows[x // 8][x % 8], highs[x // 8][x % 8]], axis=0)
            full = lap[x] + ends
            if planes[x] is not None:
                full = full + planes[x]
            out[x] = 2.0 * field[x] - old + vel[x] * full
    for x in range(16):
        product = s_out[x] * r_out[x]
        if step > 0:
            product = picture[x] + product
        if last:
            product = product + jnp.where(
                moved, jnp.where(arrives, image_come[x], F32(0.0)), image[x]
            )
        picture_out[x] = product
    if not last:
        send_faces((s_out, r_out), sends)


def distance():
    gx = lax.axis_index("gx")
    return jnp.minimum(gx, 31 - gx)


def keep_kernel(reach, after, held, got, low, high):
    half = 4 * reach
    holds = lax.rem(distance(), 2 * reach) == 0
    low[...] = jnp.where(holds, held[:half], got[:half])
    high[...] = jnp.where(holds, held[half:], got[half:])


def scatter_kernel(after, moves, owner, image, come, low, high):
    upper = lax.axis_index("gx") >= 16
    z = lax.broadcasted_iota(jnp.int32, (8, 256), 1)
    target = jnp.zeros((8, 256), jnp.int32)
    for slab in range(32):
        target = jnp.where(z // 8 == slab, owner[slab], target)
    target = jnp.where(upper, 31 - target, target) * 8 + lax.rem(z, 8)
    rows = lax.broadcasted_iota(jnp.int32, (128, 256), 0)
    pick = jnp.where(rows == target[0:1, :], F32(1.0), F32(0.0))
    tile = jnp.where(upper, come[...], image[...])
    leaving = jnp.where((moves[...] == 1.0)[None], tile, F32(0.0)).reshape(256, 256)
    slabs = lax.dot_general(
        pick, leaving, (((1,), (1,)), ((), ())), precision=HIGHEST, preferred_element_type=F32
    )
    low[...] = slabs[:64]
    high[...] = slabs[64:]


def gather_kernel(owner, held, got, base, out, token):
    gx = lax.axis_index("gx")
    mine = jnp.int32(0)
    for slab in range(32):
        mine = jnp.where(owner[slab] == gx, slab, mine)
    depth = lax.broadcasted_iota(jnp.int32, (8, 256), 0)
    z = lax.broadcasted_iota(jnp.int32, (8, 256), 1)
    spread = jnp.where(z == 8 * mine + depth, F32(1.0), F32(0.0))
    slab = jnp.where(lax.rem(distance(), 2) == 0, held[...], got[...])
    out[...] = base[...] + lax.dot_general(
        slab, spread, (((0,), (0,)), ((), ())), precision=HIGHEST, preferred_element_type=F32
    ).reshape(16, 16, 256)
    token[...] = jnp.zeros((8, 128), F32)


def body(
    courant,
    vel_entering,
    image,
    src_prev,
    src_cur,
    rcv_prev,
    rcv_cur,
    global_image,
    shift_map,
    image_owner,
):
    n, m = 32, 8
    west = [(i, (i - 1) % n) for i in range(n)]
    pair_x = [(i, i ^ 1) for i in range(n)]
    odd_x = [(i, (i + (1 if i % 2 else -1)) % n) for i in range(n)]
    pair_y = [(i, i ^ 1) for i in range(m)]
    odd_y = [(i, (i + (1 if i % 2 else -1)) % m) for i in range(m)]

    def swap(x1, od, y1, yo):
        x1 = lax.ppermute(x1, "gx", pair_x)
        od = lax.ppermute(od, "gx", odd_x)
        yo = lax.ppermute(yo, "gy", odd_y)
        y1 = lax.ppermute(y1, "gy", pair_y)
        return x1, od, y1, yo

    owner = image_owner.reshape(32)
    tile = sds(16, 16, 256)
    faces = [sds(2, 4, 16, 256), sds(2, 4, 16, 256), sds(2, 8, 8, 256), sds(2, 8, 8, 256)]
    scratch = [pltpu.VMEM((24, 32, 256), F32)] * 2 + [pltpu.VMEM((16, 16, 256), F32)] * 2

    s_come = lax.ppermute(src_cur, "gx", west)
    r_come = lax.ppermute(rcv_cur, "gx", west)
    sp_come = lax.ppermute(src_prev, "gx", west)
    rp_come = lax.ppermute(rcv_prev, "gx", west)
    (vel_send,) = call(first_kernel, [tile], [], courant, image)
    vel_come = lax.ppermute(vel_send, "gx", west)
    s_own, r_own, mask = call(
        own_kernel, [tile] * 2 + [sds(16, 256)], [], shift_map, src_cur, rcv_cur
    )
    s, r, *sends = call(
        move_kernel, [tile, tile] + faces, [], mask, s_own, r_own, s_come, r_come
    )

    for step in range(STEPS):
        last = step == STEPS - 1
        halos = swap(*sends)
        if step == 0:
            low, high = call(
                scatter_kernel,
                [sds(64, 256)] * 2,
                [],
                mask,
                owner,
                image,
                vel_come,
                after=(halos[0],),
            )
        else:
            low, high = call(
                functools.partial(keep_kernel, 16 >> step),
                [sds(64 >> step, 256)] * 2,
                [],
                low,
                got,
                after=(halos[1] if step in (1, 2,) else halos[0],),
            )
        got = lax.ppermute(high, "gx", [(i, i ^ (8 >> step)) for i in range(n)])
        s_lap, r_lap = call(interior_kernel, [tile, tile], scratch, s, r)
        if step == 2:
            (image_send,) = call(copy_kernel, [tile], [], image, after=(s_lap,))
            image_come = lax.ppermute(image_send, "gx", west)
        ins = [s, r, s_lap, r_lap, *halos]
        outs = [tile] * 3
        if step == 0:
            ins += [mask, src_prev, rcv_prev, courant, vel_entering]
            ins += [sp_come, rp_come, vel_come]
        else:
            ins += [s_old, r_old, velocity, picture]
        if last:
            global_out, token = call(
                gather_kernel, [tile, sds(8, 128)], [], owner, low, got, global_image
            )
            ins += [mask, image, image_come]
            outs = outs + [tile] * 2
        else:
            outs = outs + faces
        if step == 0:
            outs = outs + [tile]
        after = ()
        if step == 0:
            after = (got,)
        if step == 3:
            after = (token,)
        new = call(functools.partial(update_kernel, step), outs, [], *ins, after=after)
        if last:
            s_new, r_new, picture, s, r = new
            return (global_out, picture, s, s_new, r, r_new)
        s_old, r_old = s, r
        s, r, picture, *sends = new
        if step == 0:
            velocity = sends.pop()


def solution(mesh):
    tiled = P("gx", "gy", None)
    in_specs = (
        tiled,
        P(None, "gy", None),
        tiled,
        tiled,
        tiled,
        tiled,
        tiled,
        tiled,
        P("gy"),
        P("gy", None),
    )
    return jax.shard_map(
        body, mesh=mesh, in_specs=in_specs, out_specs=(tiled,) * 6, check_vma=False
    )
```

```python
import functools

import jax
import jax.numpy as jnp
from jax import lax
from jax.experimental import pallas as pl
from jax.experimental.pallas import tpu as pltpu
from jax.sharding import PartitionSpec as P

STEPS = 4
STENCIL = (-205.0 / 72.0, 8.0 / 5.0, -1.0 / 5.0, 8.0 / 315.0, -1.0 / 560.0)
F32 = jnp.float32
HIGHEST = lax.Precision.HIGHEST
LIMIT = 12 * 1024 * 1024
WAITS = (1, 0, 0, 1)


def sds(*shape):
    return jax.ShapeDtypeStruct(shape, F32)


def call(kernel, outs, scratch, *args, after=(), cost=1 << 20):
    specs = [pl.BlockSpec(memory_space=pl.ANY)] * len(after)
    for a in args:
        space = pltpu.SMEM if a.dtype == jnp.int32 else pltpu.VMEM
        specs.append(pl.BlockSpec(memory_space=space))
    return pl.pallas_call(
        kernel,
        out_shape=outs,
        in_specs=specs,
        out_specs=[pl.BlockSpec(memory_space=pltpu.VMEM)] * len(outs),
        scratch_shapes=scratch,
        compiler_params=pltpu.CompilerParams(vmem_limit_bytes=LIMIT),
        cost_estimate=pl.CostEstimate(flops=cost, bytes_accessed=cost, transcendentals=0),
    )(*after, *args)


def place():
    return lax.axis_index("gx"), lax.axis_index("gy")


def send_faces(fields, sends):
    x1, od, y1, yo = sends
    gx, gy = place()
    even_x, even_y = lax.rem(gx, 2) == 0, lax.rem(gy, 2) == 0
    toward = jnp.where(even_x, 12, 0)
    for f, field in enumerate(fields):
        x1[f] = field[pl.ds(toward, 4)]
        od[f] = field[pl.ds(12 - toward, 4)]
        for half in range(2):
            block = field[8 * half : 8 * half + 8]
            low, high = block[:, 0:4, :], block[:, 12:16, :]
            rows = slice(4 * half, 4 * half + 4)
            y1[f, :, rows, :] = jnp.where(even_y, high, low)
            yo[f, :, rows, :] = jnp.where(even_y, low, high)


def interior_kernel(s, r, s_lap, r_lap, ext_s, ext_r, depth_s, depth_r):
    i = lax.broadcasted_iota(jnp.int32, (256, 256), 0)
    j = lax.broadcasted_iota(jnp.int32, (256, 256), 1)
    apart = jnp.abs(i - j)
    matrix = jnp.where(apart == 0, F32(3.0 * STENCIL[0]), F32(0.0))
    for k in range(1, 5):
        matrix = jnp.where(apart == k, F32(STENCIL[k]), matrix)
    for field, out, ext, depth in ((s, s_lap, ext_s, depth_s), (r, r_lap, ext_r, depth_r)):
        ext[4:20, 8:24, :] = field[...]
        ext[0:4, 8:24, :] = jnp.zeros((4, 16, 256), F32)
        ext[20:24, 8:24, :] = jnp.zeros((4, 16, 256), F32)
        ext[4:20, 0:8, :] = jnp.zeros((16, 8, 256), F32)
        ext[4:20, 24:32, :] = jnp.zeros((16, 8, 256), F32)
        depth[...] = jnp.dot(
            field[...].reshape(256, 256), matrix, precision=HIGHEST, preferred_element_type=F32
        ).reshape(16, 16, 256)
        for x in range(0, 16, 2):
            lap = depth[x : x + 2]
            here, there = slice(4 + x, 6 + x), slice(8, 24)
            for k in range(1, 5):
                pair = ext[4 + x + k : 6 + x + k, there, :] + ext[4 + x - k : 6 + x - k, there, :]
                pair = pair + (ext[here, 8 + k : 24 + k, :] + ext[here, 8 - k : 24 - k, :])
                lap = lap + F32(STENCIL[k]) * pair
            out[x : x + 2] = lap


def face_terms(halos, f):
    x1, od, y1, yo = halos
    gx, gy = place()
    even_x, even_y = lax.rem(gx, 2) == 0, lax.rem(gy, 2) == 0
    zero = F32(0.0)
    a, b = x1[f], od[f]
    low = jnp.where(gx > 0, jnp.where(even_x, b, a), zero)
    high = jnp.where(gx < 31, jnp.where(even_x, a, b), zero)
    planes = [None] * 16
    for p in range(4):
        planes[p] = sum(F32(STENCIL[k]) * low[4 + p - k] for k in range(p + 1, 5))
        planes[12 + p] = sum(F32(STENCIL[k]) * high[p + k - 4] for k in range(4 - p, 5))
    a, b = y1[f], yo[f]
    low = jnp.where(gy > 0, jnp.where(even_y, b, a), zero)
    high = jnp.where(gy < 7, jnp.where(even_y, a, b), zero)
    sub = lax.broadcasted_iota(jnp.int32, (8, 8, 256), 1)
    row = lax.rem(sub, 4)
    low_sum, high_sum = F32(STENCIL[4]) * low, F32(STENCIL[4]) * high
    for k in range(1, 4):
        c = F32(STENCIL[k])
        low_sum = low_sum + jnp.where(row < k, c * pltpu.roll(low, 4 + k, axis=1), zero)
        high_sum = high_sum + jnp.where(row >= 4 - k, c * pltpu.roll(high, 4 - k, axis=1), zero)
    first = sub < 4
    lows = (jnp.where(first, low_sum, zero), jnp.where(first, pltpu.roll(low_sum, 4, axis=1), zero))
    highs = (jnp.where(first, zero, pltpu.roll(high_sum, 4, axis=1)), jnp.where(first, zero, high_sum))
    return planes, lows, highs


def move_kernel(moves, s, r, s_in, r_in, s_out, r_out, *sends):
    arrives = place()[0] < 31
    moved = (moves[...] == 1.0)
    for own, come, out in ((s, s_in, s_out), (r, r_in, r_out)):
        for x in range(0, 16, 2):
            out[x : x + 2] = jnp.where(
                moved[None], jnp.where(arrives, come[x : x + 2], F32(0.0)), own[x : x + 2]
            )
    send_faces((s_out, r_out), sends)


def own_kernel(moves, s, r, s_out, r_out, mask):
    s_out[...] = s[...]
    r_out[...] = r[...]
    row = lax.broadcasted_iota(jnp.int32, (16, 256), 0)
    flags = jnp.zeros((16, 256), jnp.int32)
    for y in range(16):
        flags = jnp.where(row == y, moves[y], flags)
    mask[...] = jnp.where(flags == 1, F32(1.0), F32(0.0))


RIM = (0, 1, 2, 3, 12, 13, 14, 15)


def rim_kernel(s, r, vel, image, s_out, r_out, vel_out):
    first = place()[0] == 0
    for j, x in enumerate(RIM):
        rows = slice(16 * j, 16 * j + 16)
        s_out[rows] = s[x]
        r_out[rows] = jnp.where(first, image[12 + j], r[x]) if j < 4 else r[x]
        vel_out[rows] = jnp.where(first, image[j], vel[x])
    for j in range(8):
        x, at, row = 4 + j, 128 + 8 * j, 8 * (j % 2)
        for part, y in ((0, 0), (4, 12)):
            rows = slice(at + part, at + part + 4)
            s_out[rows] = s[x, y : y + 4]
            r_out[rows] = r[x, y : y + 4]
            vel_out[rows] = jnp.where(
                first, image[8 + j // 2, row + part : row + part + 4], vel[x, y : y + 4]
            )


def rim_plane(rim, x):
    if x in RIM:
        at = 16 * RIM.index(x)
        return rim[at : at + 16]
    block = rim[128 + 8 * (x - 4) : 136 + 8 * (x - 4)]
    return jnp.concatenate([block, block], axis=0)


def core_kernel(after, s, r, vel, out):
    for i, ref in enumerate((s, r, vel)):
        out[i, :, 4:8, :] = ref[4:12, 4:8, :]
        out[i, :, 0:4, :] = ref[4:12, 8:12, :]


def patch_kernel(
    moves, s, r, s_lap, r_lap, s_prev, r_prev, vel_own, vel_end, come,
    s_new, r_new, vel, picture, s_out, r_out, vel_out, picture_out,
):
    moved = moves[...] == 1.0
    arrives = place()[0] < 31
    row = lax.broadcasted_iota(jnp.int32, (16, 256), 0)
    core = (row >= 4) & (row < 12)
    for x in range(16):
        if x in RIM:
            s_out[x] = s_new[x]
            r_out[x] = r_new[x]
            vel_out[x] = vel[x]
            picture_out[x] = picture[x]
            continue
        full = [jnp.concatenate([come[i, x - 4]] * 2, axis=0) for i in range(3)]
        new = jnp.where(moved, jnp.where(arrives, full[2], vel_end[x]), vel_own[x])
        vel_out[x] = jnp.where(core, new, vel[x])
        for f, (field, lap, prev, old, out) in enumerate(
            ((s, s_lap, s_prev, s_new, s_out), (r, r_lap, r_prev, r_new, r_out))
        ):
            before = jnp.where(moved, jnp.where(arrives, full[f], F32(0.0)), prev[x])
            out[x] = jnp.where(core, 2.0 * field[x] - before + new * lap[x], old[x])
        picture_out[x] = jnp.where(core, s_out[x] * r_out[x], picture[x])


def copy_kernel(after, a, out):
    out[...] = a[...]


def update_kernel(step, *refs):
    refs = list(refs)
    take = lambda n: [refs.pop(0) for _ in range(n)]
    last = step == STEPS - 1
    take(WAITS[step])
    s, r, s_lap, r_lap = take(4)
    halos = take(4)
    if step == 0:
        moves, s_prev, r_prev, vel_own, vel_end, s_come, r_come, vel_come = take(8)
    else:
        s_prev, r_prev, vel, picture = take(4)
    if last:
        moves, image, image_come = take(3)
    s_out, r_out, picture_out = take(3)
    if last:
        s_before, r_before = take(2)
    else:
        sends = take(4)
    if step == 0:
        (vel,) = take(1)

    if step == 0 or last:
        moved = (moves[...] == 1.0)
        arrives = place()[0] < 31
    if last:
        s_before[...] = s[...]
        r_before[...] = r[...]
    if step == 0:
        for x in range(16):
            new = jnp.where(arrives, rim_plane(vel_come, x), vel_end[x])
            vel[x] = jnp.where(moved, new, vel_own[x])
    if step > 0:
        s_come = r_come = None
    for f, (field, lap, prev, come, out) in enumerate(
        ((s, s_lap, s_prev, s_come, s_out), (r, r_lap, r_prev, r_come, r_out))
    ):
        planes, lows, highs = face_terms(halos, f)
        for x in range(16):
            if step == 0:
                old = jnp.where(moved, jnp.where(arrives, rim_plane(come, x), F32(0.0)), prev[x])
            else:
                old = prev[x]
            ends = jnp.concatenate([lows[x // 8][x % 8], highs[x // 8][x % 8]], axis=0)
            full = lap[x] + ends
            if planes[x] is not None:
                full = full + planes[x]
            out[x] = 2.0 * field[x] - old + vel[x] * full
    for x in range(16):
        product = s_out[x] * r_out[x]
        if step > 0:
            product = picture[x] + product
        if last:
            product = product + jnp.where(
                moved, jnp.where(arrives, image_come[x], F32(0.0)), image[x]
            )
        picture_out[x] = product
    if not last:
        send_faces((s_out, r_out), sends)


def distance():
    gx = lax.axis_index("gx")
    return jnp.minimum(gx, 31 - gx)


def keep_kernel(reach, after, held, got, low, high):
    half = 4 * reach
    holds = lax.rem(distance(), 2 * reach) == 0
    low[...] = jnp.where(holds, held[:half], got[:half])
    high[...] = jnp.where(holds, held[half:], got[half:])


def scatter_kernel(after, moves, owner, image, most, rest, low, high):
    upper = lax.axis_index("gx") >= 16
    z = lax.broadcasted_iota(jnp.int32, (8, 256), 1)
    target = jnp.zeros((8, 256), jnp.int32)
    for slab in range(32):
        target = jnp.where(z // 8 == slab, owner[slab], target)
    target = jnp.where(upper, 31 - target, target) * 8 + lax.rem(z, 8)
    rows = lax.broadcasted_iota(jnp.int32, (128, 256), 0)
    pick = jnp.where(rows == target[0:1, :], F32(1.0), F32(0.0))
    end = jnp.concatenate([most[...], rest[:64]], axis=0)
    tile = jnp.where(upper, end, image[...].reshape(256, 256))
    leaves = jnp.broadcast_to((moves[...] == 1.0)[None], (16, 16, 256)).reshape(256, 256)
    leaving = jnp.where(leaves, tile, F32(0.0))
    slabs = lax.dot_general(
        pick, leaving, (((1,), (1,)), ((), ())), precision=HIGHEST, preferred_element_type=F32
    )
    low[...] = slabs[:64]
    high[...] = slabs[64:]


def gather_kernel(owner, held, got, base, out, token):
    gx = lax.axis_index("gx")
    mine = jnp.int32(0)
    for slab in range(32):
        mine = jnp.where(owner[slab] == gx, slab, mine)
    depth = lax.broadcasted_iota(jnp.int32, (8, 256), 0)
    z = lax.broadcasted_iota(jnp.int32, (8, 256), 1)
    spread = jnp.where(z == 8 * mine + depth, F32(1.0), F32(0.0))
    slab = jnp.where(lax.rem(distance(), 2) == 0, held[...], got[...])
    out[...] = base[...] + lax.dot_general(
        slab, spread, (((0,), (0,)), ((), ())), precision=HIGHEST, preferred_element_type=F32
    ).reshape(16, 16, 256)
    token[...] = jnp.zeros((8, 128), F32)


def body(
    courant,
    vel_entering,
    image,
    src_prev,
    src_cur,
    rcv_prev,
    rcv_cur,
    global_image,
    shift_map,
    image_owner,
):
    n, m = 32, 8
    west = [(i, (i - 1) % n) for i in range(n)]
    pair_x = [(i, i ^ 1) for i in range(n)]
    odd_x = [(i, (i + (1 if i % 2 else -1)) % n) for i in range(n)]
    pair_y = [(i, i ^ 1) for i in range(m)]
    odd_y = [(i, (i + (1 if i % 2 else -1)) % m) for i in range(m)]

    def swap(x1, od, y1, yo):
        x1 = lax.ppermute(x1, "gx", pair_x)
        od = lax.ppermute(od, "gx", odd_x)
        yo = lax.ppermute(yo, "gy", odd_y)
        y1 = lax.ppermute(y1, "gy", pair_y)
        return x1, od, y1, yo

    owner = image_owner.reshape(32)
    tile = sds(16, 16, 256)
    faces = [sds(2, 4, 16, 256), sds(2, 4, 16, 256), sds(2, 8, 8, 256), sds(2, 8, 8, 256)]
    scratch = [pltpu.VMEM((24, 32, 256), F32)] * 2 + [pltpu.VMEM((16, 16, 256), F32)] * 2

    s_come = lax.ppermute(src_cur, "gx", west)
    r_come = lax.ppermute(rcv_cur, "gx", west)
    rims = call(rim_kernel, [sds(192, 256)] * 3, [], src_prev, rcv_prev, courant, image)
    vel_come, sp_come, rp_come = [lax.ppermute(rims[i], "gx", west) for i in (2, 0, 1)]
    s_own, r_own, mask = call(
        own_kernel, [tile] * 2 + [sds(16, 256)], [], shift_map, src_cur, rcv_cur
    )
    s, r, *sends = call(
        move_kernel, [tile, tile] + faces, [], mask, s_own, r_own, s_come, r_come
    )

    for step in range(STEPS):
        last = step == STEPS - 1
        halos = swap(*sends)
        if step == 0:
            low, high = call(
                scatter_kernel,
                [sds(64, 256)] * 2,
                [],
                mask,
                owner,
                image,
                vel_come,
                rp_come,
                after=(halos[0],),
            )
        else:
            low, high = call(
                functools.partial(keep_kernel, 16 >> step),
                [sds(64 >> step, 256)] * 2,
                [],
                low,
                got,
                after=(halos[1] if step in (1, 2,) else halos[0],),
            )
        got = lax.ppermute(high, "gx", [(i, i ^ (8 >> step)) for i in range(n)])
        if step == 1:
            s, r, velocity, picture = call(
                patch_kernel,
                [tile] * 4,
                [],
                mask,
                s_old,
                r_old,
                s_lap,
                r_lap,
                src_prev,
                rcv_prev,
                courant,
                vel_entering,
                core_come,
                s,
                r,
                velocity,
                picture,
            )
        s_lap, r_lap = call(interior_kernel, [tile, tile], scratch, s, r)
        if step == 0:
            (core,) = call(
                core_kernel, [sds(3, 8, 8, 256)], [], src_prev, rcv_prev, courant, after=(s_lap,)
            )
            core_come = lax.ppermute(core, "gx", west)
        if step == 2:
            (image_send,) = call(copy_kernel, [tile], [], image, after=(s_lap,))
            image_come = lax.ppermute(image_send, "gx", west)
        ins = [s, r, s_lap, r_lap, *halos]
        outs = [tile] * 3
        if step == 0:
            ins += [mask, src_prev, rcv_prev, courant, vel_entering]
            ins += [sp_come, rp_come, vel_come]
        else:
            ins += [s_old, r_old, velocity, picture]
        if last:
            global_out, token = call(
                gather_kernel, [tile, sds(8, 128)], [], owner, low, got, global_image
            )
            ins += [mask, image, image_come]
            outs = outs + [tile] * 2
        else:
            outs = outs + faces
        if step == 0:
            outs = outs + [tile]
        after = ()
        if step == 0:
            after = (got,)
        if step == 3:
            after = (token,)
        new = call(functools.partial(update_kernel, step), outs, [], *ins, after=after)
        if last:
            s_new, r_new, picture, s, r = new
            return (global_out, picture, s, s_new, r, r_new)
        s_old, r_old = s, r
        s, r, picture, *sends = new
        if step == 0:
            velocity = sends.pop()


def solution(mesh):
    tiled = P("gx", "gy", None)
    in_specs = (
        tiled,
        P(None, "gy", None),
        tiled,
        tiled,
        tiled,
        tiled,
        tiled,
        tiled,
        P("gy"),
        P("gy", None),
    )
    return jax.shard_map(
        body, mesh=mesh, in_specs=in_specs, out_specs=(tiled,) * 6, check_vma=False
    )
```
